1024 devices in a mesh: dp: 16 (over y, core), rows: 64 (over z, x).
Axes of the slice: x: 4, y: 8, z: 16, core: 2. Of those that a mesh axis runs over, the one named last changes fastest.
Arguments:
- item_table: float32 [131072, 256], P('rows'), may hold values from -0.5 to 0.5
- row_accum: float32 [131072], P('rows'), may hold values from 0.1 to 10
- owner_map: int32 [16, 64, 512, 1], P('dp', 'rows'), may hold values from 0 to 63; in each aligned block of 512 rows (0 to 511, 512 to 1023, ..., all dimensions but the last counted through in order) at most 24 rows name the same one
- row_index: int32 [16, 64, 512], P('dp', 'rows'), may hold values from 0 to 2047
- bag_index: int32 [16, 64, 512], P('dp', 'rows'), may hold values from 0 to 3, never falling along the last dimension, each value on 1 to 256 neighbouring positions
- prev_owner: int32 [16, 64, 512, 1], P('dp', 'rows'), may hold values from 0 to 63; in each aligned block of 512 rows (0 to 511, 512 to 1023, ..., all dimensions but the last counted through in order) at most 24 rows name the same one
- prev_row: int32 [16, 64, 512], P('dp', 'rows'), may hold values from 0 to 2047
- prev_bag: int32 [16, 64, 512], P('dp', 'rows'), may hold values from 0 to 3, never falling along the last dimension, each value on 1 to 256 neighbouring positions
- grad_pooled: float32 [16, 64, 4, 256], P('dp', 'rows'), may hold values from -6 to 6
Outputs:
- pooled: float32 [16, 64, 4, 256], P('dp', 'rows')
- new_table: float32 [131072, 256], P('rows')
- new_accum: float32 [131072], P('rows')
The draws below stay inside these ranges and needn't reach their ends.
Inputs may be any that keep to these rules, and one draw needn't show every extreme that they name: `owner_map`: among the positions of one device no owner is named more than 24 times, a bound that some block reaches. `prev_owner`: among the positions of one device no owner is named more than 24 times, a bound that some block reaches. `bag_index`: never falls along a device's positions; every bag has 1 to 256 positions, one exactly 256. `prev_bag`: never falls along a device's positions; every bag has 1 to 256 positions, one exactly 256.
All inputs are finite; a program needn't handle non-finite values.
Results may differ from the reference program's by a relative error of at most 0.0003.
Values sent between devices are 32-bit elements; how exact they have to be, the bound alone decides.
A program may use at most 32 MiB of HBM per device.

```python
import math
import jax
import jax.numpy as jnp
import numpy as np
from jax import lax

E = 256
ROWS_DEV = 2048
BAGS = 4
BAG_MEAN = 128
P_SIZE = 512
BAG_MAX = 256
GROUPS = 16
OWNERS = 64
SLAB = 131072
CAP = 24


def plant(values, rng, least, top_value):
    spot = [jax.random.randint(jax.random.fold_in(rng, axis), (), 0, length) for axis, length in enumerate(values.shape)]
    longest = values.shape.index(max(values.shape))
    beside = spot[:longest] + [(spot[longest] + 1) % values.shape[longest]] + spot[longest + 1:]
    return values.at[tuple(spot)].set(least).at[tuple(beside)].set(top_value)


def block_scale(key, extent, split, low, largest):
    factor_of, own = 1.0, jax.random.fold_in(key, 6)
    for position, shards_of in split:
        heights = jnp.exp(jax.random.uniform(jax.random.fold_in(own, position), (shards_of,), jnp.float32, low / len(split), largest / len(split)))
        factor_of = factor_of * jnp.repeat(heights, extent[position] // shards_of).reshape([-1 if axis == position else 1 for axis in range(len(extent))])
    return factor_of


def profile(amount, total, reach, lean):
    weights = [(1 << 20) // math.isqrt(grade ** lean) + 1 for grade in range(2, amount + 1)]
    surplus, given = total - reach - (amount - 1), [1] * (amount - 1)
    while surplus > 0:
        free = [i for i in range(amount - 1) if given[i] < reach]
        whole, remaining = sum([weights[i] for i in free]), surplus
        for i in free:
            extra = min(reach - given[i], max(1, remaining * weights[i] // whole), surplus)
            given[i] = given[i] + extra
            surplus = surplus - extra
    return np.array([reach] + given)


def uneven_parts(key, count, total, limit, slope):
    if count == 2:
        one = jax.random.randint(key, (), max(1, total - limit), min(limit, total - 1) + 1)
        return jnp.stack([one, total - one])
    sizes = jnp.asarray(profile(count, total, limit, slope), jnp.int32)
    couples = (count - 1) // 2
    donor, receiver = sizes[1:1 + 2 * couples:2], sizes[2:2 + 2 * couples:2]
    slack = jnp.minimum(donor - 1, limit - receiver)
    passed = jax.random.randint(jax.random.fold_in(key, 1), (couples,), 0, 1 << 20) % (slack + 1)
    sizes = sizes.at[1:1 + 2 * couples:2].set(donor - passed).at[2:2 + 2 * couples:2].set(receiver + passed)
    return sizes[jax.random.permutation(jax.random.fold_in(key, 2), count)]


def assign_block(own_key, own, number, rows, amount, top, reach, skew):
    order = jax.random.permutation(own_key, amount)
    packed, ordinary = load_shares(amount, rows * top, reach, skew, True), load_shares(amount, rows * top, reach, skew, False)
    places = jnp.arange(amount)

    def named(lengths, rotation):
        used = int((lengths > 0).sum())
        fixed = max(1, used // 4)
        passed = fixed + (places - fixed + rotation * (used - fixed)) % max(1, amount - fixed)
        return jnp.zeros((amount,), jnp.int32).at[order[jnp.where(places < fixed, places, passed)]].set(jnp.asarray(lengths, jnp.int32))

    lengths = jnp.where(number % 4 == 0, named(packed, number // 4), named(ordinary, number - number // 4 - 1))
    mixed = jax.random.permutation(jax.random.fold_in(own, 3), amount)
    giver, taker = mixed[0:amount // 2 * 2:2], mixed[1:amount // 2 * 2:2]
    slack = jnp.minimum(lengths[giver] - 1, reach - lengths[taker]) // 2
    slack = jnp.where((giver == order[0]) | (taker == order[0]) | (lengths[taker] == 0), 0, jnp.maximum(slack, 0))
    passed = jax.random.randint(jax.random.fold_in(own, 4), (amount // 2,), 0, 1 << 20) % (slack + 1)
    lengths = lengths.at[giver].add(-passed).at[taker].add(passed)
    members = jnp.searchsorted(jnp.cumsum(lengths), jnp.arange(rows * top), side="right").astype(jnp.int32)
    listing = members.reshape(top, rows).T
    listing = listing[jax.random.permutation(jax.random.fold_in(own, 1), rows)]
    rotation = jax.random.randint(jax.random.fold_in(own, 2), (rows, 1), 0, top)
    return jnp.take_along_axis(listing, (jnp.arange(top)[None, :] + rotation) % top, axis=1)


def load_shares(amount, total, bound, lean, full):
    weights = [(1 << 20) // math.isqrt(grade ** lean) + 1 for grade in range(1, amount + 1)]
    largest = bound if full else min(bound, max(-(-total // amount), total * weights[0] // sum(weights)))
    least = 1 if total - largest >= amount - 1 else 0
    counts, surplus = [largest] + [least] * (amount - 1), total - largest - least * (amount - 1)
    while surplus > 0:
        candidates = [i for i in range(1, amount) if counts[i] < largest] or [i for i in range(1, amount) if counts[i] < bound]
        mass, left = sum([weights[i] for i in candidates]), surplus
        for i in candidates:
            addition = min(bound - counts[i], max(1, left * weights[i] // mass), surplus)
            counts[i] = counts[i] + addition
            surplus = surplus - addition
    return np.array(counts)


def scatter_about(own_key, shape, width, limit, shards=(), dtype=jnp.bfloat16):
    entries = jax.random.normal(own_key, shape, jnp.float32) * width
    if len(shards) > 0:
        entries = block_scale(own_key, shape, shards, -0.22, 0.18) * entries
    return jnp.clip(entries, min=-limit, max=limit).astype(dtype)


def setup_inputs(seed: int = 0) -> dict:
    splits = jax.random.split(jax.random.key(seed), 10)
    item_table = scatter_about(splits[0], (SLAB, E), BAG_MEAN ** -0.5, 0.5, ((0, 64),), jnp.float32)
    row_accum = jnp.clip(jnp.exp(math.log(10.0) - 4.6051702 * jax.random.uniform(splits[1], (SLAB,), jnp.float32) ** block_scale(splits[1], (SLAB,), ((0, 64),), -0.2, 0.2)), 0.1, 10.0)
    owner_map_keys = jax.random.split(jax.random.fold_in(splits[2], 1), GROUPS * OWNERS * P_SIZE // P_SIZE)
    owner_map_turns = jax.random.permutation(jax.random.fold_in(splits[2], 3), GROUPS * OWNERS * P_SIZE // P_SIZE)
    owner_map = jax.vmap(lambda own, number: assign_block(jax.random.fold_in(splits[2], 2), own, number, P_SIZE, OWNERS, 1, CAP, 2))(owner_map_keys, owner_map_turns).reshape((GROUPS, OWNERS, P_SIZE, 1))
    row_index = plant(jax.random.randint(splits[3], (GROUPS, OWNERS, P_SIZE), 0, ROWS_DEV), jax.random.fold_in(splits[3], 1), 0, ROWS_DEV - 1).astype(jnp.int32)
    bag_index = jax.vmap(lambda own: jnp.searchsorted(jnp.cumsum(uneven_parts(own, BAGS, P_SIZE, BAG_MAX, 2)), jnp.arange(P_SIZE), side="right"))(jax.random.split(splits[4], GROUPS * OWNERS)).reshape((GROUPS, OWNERS, P_SIZE)).astype(jnp.int32)
    prev_owner_keys = jax.random.split(jax.random.fold_in(splits[5], 1), GROUPS * OWNERS * P_SIZE // P_SIZE)
    prev_owner_turns = jax.random.permutation(jax.random.fold_in(splits[5], 3), GROUPS * OWNERS * P_SIZE // P_SIZE)
    prev_owner = jax.vmap(lambda own, number: assign_block(jax.random.fold_in(splits[5], 2), own, number, P_SIZE, OWNERS, 1, CAP, 2))(prev_owner_keys, prev_owner_turns).reshape((GROUPS, OWNERS, P_SIZE, 1))
    prev_row = plant(jax.random.randint(splits[6], (GROUPS, OWNERS, P_SIZE), 0, ROWS_DEV), jax.random.fold_in(splits[6], 1), 0, ROWS_DEV - 1).astype(jnp.int32)
    prev_bag = jax.vmap(lambda own: jnp.searchsorted(jnp.cumsum(uneven_parts(own, BAGS, P_SIZE, BAG_MAX, 2)), jnp.arange(P_SIZE), side="right"))(jax.random.split(splits[7], GROUPS * OWNERS)).reshape((GROUPS, OWNERS, P_SIZE)).astype(jnp.int32)
    grad_pooled = scatter_about(splits[8], (GROUPS, OWNERS, BAGS, E), 1.0, 6.0, ((0, 16), (1, 64)), jnp.float32)
    return {"item_table": item_table, "row_accum": row_accum, "owner_map": owner_map, "row_index": row_index, "bag_index": bag_index, "prev_owner": prev_owner, "prev_row": prev_row, "prev_bag": prev_bag, "grad_pooled": grad_pooled}


learn_rate = 0.1

def reference(item_table, row_accum, owner_map, row_index, bag_index, prev_owner, prev_row, prev_bag, grad_pooled):
    owner_range = jnp.arange(OWNERS).astype(jnp.int32)

    def pool_group(operands):
        owners_now, rows_now, bags_now = operands
        slab_index = (owners_now[..., 0] * ROWS_DEV + rows_now).astype(jnp.int32)
        looked = item_table[slab_index.reshape(-1)]
        segment = (bags_now + BAGS * owner_range[:, None]).astype(jnp.int32).reshape(-1)
        summed = jax.ops.segment_sum(looked, segment, num_segments=OWNERS * BAGS)
        return summed.reshape(OWNERS, BAGS, E)
    pooled = lax.map(pool_group, (owner_map, row_index, bag_index))

    def add_group(running, operands):
        owners_old, rows_old, bags_old, grad_group = operands
        slab_index = (owners_old[..., 0] * ROWS_DEV + rows_old).astype(jnp.int32).reshape(-1)
        grad_each = grad_group[owner_range[:, None], bags_old].reshape(-1, E)
        return (running + jax.ops.segment_sum(grad_each, slab_index, num_segments=SLAB), None)
    grad_rows, _ = lax.scan(add_group, jnp.zeros((SLAB, E), jnp.float32), (prev_owner, prev_row, prev_bag, grad_pooled))
    new_accum = row_accum + lax.optimization_barrier(jnp.mean(grad_rows * grad_rows, axis=1))
    new_table = item_table - learn_rate * grad_rows / jnp.sqrt(new_accum)[:, None]
    return (pooled, new_table, new_accum)
```

```python
import functools

import jax
import jax.numpy as jnp
from jax import lax
from jax.experimental import pallas as pl
from jax.experimental.pallas import tpu as pltpu
from jax.sharding import PartitionSpec as P

learn_rate = 0.1
CAP = 24
NX = 4
MESH = pl.DeviceIdType.MESH
F32, BF16, I32 = jnp.float32, jnp.bfloat16, jnp.int32
NT = (((1,), (1,)), ((), ()))
NN = (((1,), (0,)), ((), ()))


def dot(a, b, dims=NN):
    return lax.dot_general(a, b, dims, preferred_element_type=F32)


def iota(shape, axis):
    return lax.broadcasted_iota(I32, shape, axis)


def split(v):
    high = v.astype(BF16)
    return high, (v - high.astype(F32)).astype(BF16)


def one_hot(mask):
    return jnp.where(mask, 1.0, 0.0).astype(BF16)


def by_owner(owner, row, bag, powner, prow, pbag, nz):
    n = owner.shape[1]

    def owners(o):
        return iota((nz * 8, n), 0) == (o // NX) * 8 + o % NX

    mine, old = owners(owner), owners(powner)
    both = jnp.concatenate([one_hot(mine), one_hot(old)], axis=0)
    before = one_hot(iota((n, n), 0) < iota((n, n), 1))
    count = dot(both, before)

    def places(mask, count, row, bag):
        rank = jnp.sum(jnp.where(mask, count, 0.0), axis=0, keepdims=True)
        hit = iota((32, n), 0).astype(F32) == rank
        row = row + 1
        low, high, bag = (v.astype(F32) for v in (row % 128, row // 128, bag))
        pick = lambda v: jnp.where(hit, v, 0.0)
        return pick(low), pick(high), pick(bag)

    low, high, bags = places(mine, count[: nz * 8], row, bag)
    plow, phigh, pbags = places(old, count[nz * 8:], prow, pbag)
    none, none2 = jnp.zeros((64, n), F32), jnp.zeros((32, n), F32)
    cat = functools.partial(jnp.concatenate, axis=0)
    lows = jnp.concatenate([cat([low, bags, none]), cat([none, plow, pbags])], axis=1)
    highs = jnp.concatenate([cat([high, none2, none]), cat([none, phigh, none2])], axis=1)
    left = jnp.concatenate([both[: nz * 8], both[nz * 8:]], axis=1)
    return dot(left, lows.astype(BF16), NT) + 128.0 * dot(left, highs.astype(BF16), NT)


def kernel(
    ny, nz,
    owner, row, bag, powner, prow, pbag, grad, accum, table,
    pooled, new_table, new_accum,
    tab, tabs, zsend, zbuf, xsend, xbuf, expand, hits, look, part, psend, pbuf, qsend, qbuf,
    u, rbuf, gall, tout, nacc,
    tab_sem, out_sem, z_sem, x_send, x_recv, c_send, c_recv,
    rs_send, rs_recv, ag_send, ag_recv, k_send, k_recv, px_send, px_recv, pz_sem,
):
    dp, rw = lax.axis_index("dp"), lax.axis_index("rows")
    y, c, z, x = dp // 2, dp % 2, rw // NX, rw % NX
    ns = NX * nz
    rows_dev = tab.shape[0]
    half_rows = rows_dev // 2
    nb = half_rows // ny
    nh = nb // 2
    gt = nz * 8

    def at(dp_, rw_):
        return {"dp": dp_, "rows": rw_}

    def z_peer(d):
        return at(dp, ((z + d) % nz) * NX + x)

    def x_peer(d):
        return at(dp, z * NX + (x + d) % NX)

    partner = at(y * 2 + 1 - c, rw)
    y_peer = [at(((y + 1) % ny) * 2 + c, rw), at(((y + ny - 1) % ny) * 2 + c, rw)]

    def remote(src, dst, s, r, dev):
        return pltpu.make_async_remote_copy(
            src_ref=src, dst_ref=dst, send_sem=s, recv_sem=r, device_id=dev, device_id_type=MESH
        )

    load = pltpu.make_async_copy(table, tab, tab_sem)
    load.start()
    barrier = pltpu.get_barrier_semaphore()

    def greet(d, _):
        pl.semaphore_signal(barrier, inc=1, device_id=z_peer(d), device_id_type=MESH)
        return 0

    lax.fori_loop(1, nz, greet, 0)
    for d in range(1, NX):
        pl.semaphore_signal(barrier, inc=1, device_id=x_peer(d), device_id_type=MESH)
    for dev in [partner] + y_peer:
        pl.semaphore_signal(barrier, inc=1, device_id=dev, device_id_type=MESH)

    message = by_owner(
        owner[...], row[...], bag[...], powner[...], prow[...], pbag[...], nz
    )
    g4 = grad[...]
    tile = jnp.concatenate([g4[:, :128], g4[:, 128:]], axis=0)
    for i in range(nz):
        zsend[i, 0:8, :] = tile
        zsend[i, 8:16, :] = message[i * 8:(i + 1) * 8]
    pl.semaphore_wait(barrier, nz - 1 + NX - 1 + 1 + 2)

    def send_z(d, _):
        to = (z + d) % nz
        remote(zsend.at[to], zbuf.at[z], z_sem.at[0], z_sem.at[1], z_peer(d)).start()
        return 0

    lax.fori_loop(1, nz, send_z, 0)
    zbuf[z] = zsend[z]
    others = zbuf.at[pl.ds(0, nz - 1)]
    z_all = remote(others, others, z_sem.at[0], z_sem.at[1], z_peer(1))
    z_all.wait_recv()

    for i in range(NX):
        for j in range(nz):
            xsend[i, j * 8:(j + 1) * 8, :] = zbuf[j, 0:8, :]
        xsend[i, gt:gt + nz, :] = zbuf[:, 8 + i, :]
    x_copies = []
    for d in range(1, NX):
        x_copies.append(
            remote(xsend.at[(x + d) % NX], xbuf.at[c, x], x_send.at[d], x_recv.at[d], x_peer(d))
        )
        x_copies[-1].start()
    xbuf[c, x] = xsend[x]
    c_copies = []
    for d in range(NX):
        if d > 0:
            x_copies[d - 1].wait_recv()
        piece = xbuf.at[c, (x + NX - d) % NX]
        c_copies.append(remote(piece, piece, c_send.at[d], c_recv.at[d], partner))
        c_copies[-1].start()

    load.wait()
    high, low = split(tab[...])
    tabs[:, 0:256] = high
    tabs[:, 256:512] = low
    for copy in c_copies:
        copy.wait_recv()

    ids = jnp.concatenate([xbuf[i, j, gt:gt + nz, :] for i in range(2) for j in range(NX)], axis=0)
    lines = 2 * ns
    grads = []
    for b in range(4):
        sides = [
            jnp.concatenate(
                [
                    xbuf[i, j, pl.ds(b + 4 * h, nz, stride=8), :]
                    for i in range(2)
                    for j in range(NX)
                ],
                axis=0,
            )
            for h in range(2)
        ]
        grads.append(jnp.concatenate(sides, axis=1))
    for k in range(CAP):
        of = ids[:, 96 + k:97 + k]
        each = jnp.where(of < 0.5, grads[0], jnp.where(of < 1.5, grads[1], jnp.where(of < 2.5, grads[2], grads[3])))
        high, low = split(each)
        expand[k * lines:(k + 1) * lines, 0:256] = high
        expand[k * lines:(k + 1) * lines, 256:512] = low
    keys = ids.T[64:64 + CAP]

    def sums(offsets):
        for i, d in enumerate(offsets):
            base = c * half_rows + ((y + d + ny) % ny) * nb + 1
            number = (iota((nb, lines), 0) + base).astype(F32)
            for k in range(CAP):
                hits[i * nb:(i + 1) * nb, k * lines:(k + 1) * lines] = one_hot(number == keys[k:k + 1, :])
        both = dot(hits[...], expand[...])
        total = both[:, 0:256] + both[:, 256:512]
        for i, d in enumerate(offsets):
            u[(d + ny) % ny] = total[i * nb:(i + 1) * nb]

    mine = jnp.concatenate([xbuf[c, j, gt:gt + nz, :] for j in range(NX)], axis=0)
    slots = CAP // 3

    def look_up(first):
        for k in range(slots):
            col = mine[:, first + k:first + k + 1]
            number = (iota((ns, rows_dev), 1) + 1).astype(F32)
            look[k * ns:(k + 1) * ns, :] = one_hot(number == col)
        both = dot(look[...], tabs[...])
        found = both[:, 0:256] + both[:, 256:512]
        for b in range(4):
            total = jnp.zeros((ns, 256), F32) if first == 0 else part[b]
            for k in range(slots):
                of = mine[:, 32 + first + k:33 + first + k]
                total = total + jnp.where(of == b, found[k * ns:(k + 1) * ns], 0.0)
            part[b] = total

    def cut(ref, h):
        return ref.at[pl.ds(h * nh, nh)]

    half = ny // 2
    pieces = [(1, 0)] + [(t, h) for t in range(2, half + 1) for h in (1, 0)]
    number_of = {piece: i for i, piece in enumerate(pieces)}
    rs_copies = {}

    def rs_copy(way, t, h):
        i = number_of[(t, h)]
        d = half + 1 - t
        src = cut(u.at[d if way == 0 else (ny - d) % ny], h if way == 0 else 1 - h)
        copy = remote(src, rbuf.at[way, i], rs_send.at[way, i], rs_recv.at[way, i], y_peer[way])
        rs_copies[way, t, h] = copy
        copy.start()

    def rs_take(way, t, h):
        rs_copies[way, t, h].wait_recv()
        i = number_of[(t, h)]
        d = half - t
        hh = h if way == 0 else 1 - h
        slot = d if way == 0 else (ny - d) % ny
        rows = pl.ds(hh * nh, nh)
        u[slot, rows, :] = u[slot, rows, :] + rbuf[way, i]

    sums((half, 0))
    for way in range(2):
        rs_copy(way, 1, 0)
    pool_steps = 0
    for t in range(2, half + 1):
        d = half + 1 - t
        sums((d, -d))
        for way in range(2):
            if t == 2:
                rs_copy(way, t, 1)
        for h in (1, 0) if t > 2 else (0,):
            for way in range(2):
                rs_take(way, t - 1, h)
                rs_copy(way, t, h)
        if pool_steps < 3:
            look_up(pool_steps * slots)
            pool_steps += 1
    while pool_steps < 3:
        look_up(pool_steps * slots)
        pool_steps += 1

    for b in range(4):
        total = part[b]
        for h in range(2):
            psend[pl.ds(b + 4 * h, ns, stride=8), :] = total[:, h * 128:(h + 1) * 128]
    px_copies = []
    for d in range(1, NX):
        src = psend.at[pl.ds(((x + d) % NX) * gt, gt)]
        px_copies.append(remote(src, pbuf.at[d], px_send.at[d], px_recv.at[d], x_peer(d)))
        px_copies[-1].start()

    for h in (1, 0):
        for way in range(2):
            rs_take(way, half, h)

    def block(line, core, h):
        return pl.ds(core * half_rows + line * nb + h * nh, nh)

    def from_line(way, t):
        return (y + ny - t) % ny if way == 0 else (y + t) % ny

    ag_copies, k_copies = {}, {}

    def ag_copy(way, t, h):
        rows = gall.at[block(from_line(way, t - 1), c, h)]
        i = (t - 1) * 2 + h
        ag_copies[way, t, h] = remote(rows, rows, ag_send.at[way, i], ag_recv.at[way, i], y_peer[way])
        ag_copies[way, t, h].start()

    def core_copy(way, t, h):
        rows = gall.at[block(from_line(way, t), c, h)]
        i = t * 2 + h
        k_copies[way, t, h] = remote(rows, rows, k_send.at[way, i], k_recv.at[way, i], partner)
        k_copies[way, t, h].start()

    def goes(way, t, h):
        return t < half or (t == half and h == way)

    for h in range(2):
        gall[block(y, c, h), :] = u[0, h * nh:(h + 1) * nh, :]
    for h in range(2):
        for way in range(2):
            if goes(way, 1, h if way == 0 else 1 - h):
                ag_copy(way, 1, h if way == 0 else 1 - h)
    for h in range(2):
        core_copy(0, 0, h)

    out_copies = []

    def update(way, t, h, core):
        line = from_line(way, t)
        rows = block(line, core, h)
        g = gall[rows, :]
        at_row = core * ny + line
        eye = iota((nh, nb), 0) + h * nh == iota((nh, nb), 1)
        before = jnp.sum(jnp.where(eye, accum[pl.ds(at_row, 1), :], 0.0), axis=1, keepdims=True)
        after = before + jnp.sum(g * g, axis=1, keepdims=True) * (1.0 / g.shape[1])
        tout[rows, :] = tab[rows, :] - learn_rate * g / jnp.sqrt(after)
        nacc[h, pl.ds(at_row, 1), :] = jnp.sum(jnp.where(eye, after, 0.0), axis=0, keepdims=True)
        pltpu.make_async_copy(tout.at[rows], new_table.at[rows], out_sem).start()

    for h in range(2):
        update(0, 0, h, c)

    for copy in px_copies:
        copy.wait_recv()
    total = psend[pl.ds(x * gt, gt), :]
    for d in range(1, NX):
        total = total + pbuf[d]
    for i in range(nz):
        qsend[i] = total[i * 8:(i + 1) * 8]

    def send_q(d, _):
        to = (z + d) % nz
        remote(qsend.at[to], qbuf.at[z], pz_sem.at[0], pz_sem.at[1], z_peer(d)).start()
        return 0

    lax.fori_loop(1, nz, send_q, 0)
    qbuf[z] = qsend[z]

    late = [(0, 0, 0), (0, 0, 1)]
    for t in range(1, half + 1):
        came = []
        for h in range(2):
            for way in range(2):
                hh = h if way == 0 else 1 - h
                if goes(way, t, hh):
                    ag_copies[way, t, hh].wait_recv()
                    if goes(way, t + 1, hh):
                        ag_copy(way, t + 1, hh)
                    core_copy(way, t, hh)
                    came.append((way, t, hh))
        for way, tt, h in came:
            update(way, tt, h, c)
        for way, tt, h in late:
            k_copies[way, tt, h].wait_recv()
            update(way, tt, h, 1 - c)
        late = came
    q_others = qbuf.at[pl.ds(0, nz - 1)]
    q_all = remote(q_others, q_others, pz_sem.at[0], pz_sem.at[1], z_peer(1))
    q_all.wait_recv()
    total = qbuf[0]
    for i in range(1, nz):
        total = total + qbuf[i]
    pooled[:, 0:128] = total[0:4]
    pooled[:, 128:256] = total[4:8]
    for way, tt, h in late:
        k_copies[way, tt, h].wait_recv()
        update(way, tt, h, 1 - c)
    new_accum[...] = nacc[0] + nacc[1]

    pltpu.make_async_copy(tout, new_table, out_sem).wait()
    z_all.wait_send()
    q_all.wait_send()
    for copy in x_copies + c_copies + px_copies:
        copy.wait_send()
    for copies in (rs_copies, ag_copies, k_copies):
        for copy in copies.values():
            copy.wait_send()


def local(
    ny, nz,
    item_table, row_accum, owner_map, row_index, bag_index, prev_owner, prev_row, prev_bag, grad_pooled,
):
    rows_dev, width = item_table.shape
    bags = grad_pooled.shape[2]
    n = row_index.shape[2]
    half_rows = rows_dev // 2
    nb = half_rows // ny
    nh = nb // 2
    ns, gt, half = NX * nz, nz * 8, ny // 2
    lines = 2 * ns
    line = lambda a: a.reshape(1, n)
    vmem = pl.BlockSpec(memory_space=pltpu.VMEM)
    hbm = pl.BlockSpec(memory_space=pl.ANY)
    dma = pltpu.SemaphoreType.DMA
    pooled, new_table, new_accum = pl.pallas_call(
        functools.partial(kernel, ny, nz),
        out_shape=[
            jax.ShapeDtypeStruct((bags, width), F32),
            jax.ShapeDtypeStruct((rows_dev, width), F32),
            jax.ShapeDtypeStruct((rows_dev // nb, nb), F32),
        ],
        in_specs=[vmem] * 8 + [hbm],
        out_specs=[vmem, hbm, vmem],
        scratch_shapes=[
            pltpu.VMEM((rows_dev, width), F32),
            pltpu.VMEM((rows_dev, 2 * width), BF16),
            pltpu.VMEM((nz, 16, 128), F32),
            pltpu.VMEM((nz, 16, 128), F32),
            pltpu.VMEM((NX, gt + nz, 128), F32),
            pltpu.VMEM((2, NX, gt + nz, 128), F32),
            pltpu.VMEM((CAP * lines, 2 * width), BF16),
            pltpu.VMEM((2 * nb, CAP * lines), BF16),
            pltpu.VMEM((CAP // 3 * ns, rows_dev), BF16),
            pltpu.VMEM((4, ns, width), F32),
            pltpu.VMEM((ns * 8, 128), F32),
            pltpu.VMEM((NX, gt, 128), F32),
            pltpu.VMEM((nz, 8, 128), F32),
            pltpu.VMEM((nz, 8, 128), F32),
            pltpu.VMEM((ny, nb, width), F32),
            pltpu.VMEM((2, 2 * half - 1, nh, width), F32),
            pltpu.VMEM((rows_dev, width), F32),
            pltpu.VMEM((rows_dev, width), F32),
            pltpu.VMEM((2, rows_dev // nb, nb), F32),
            dma(()), dma(()), dma((2,)),
            dma((NX,)), dma((NX,)), dma((NX,)), dma((NX,)),
            dma((2, 2 * half)), dma((2, 2 * half)),
            dma((2, 2 * half)), dma((2, 2 * half)),
            dma((2, 2 * half + 2)), dma((2, 2 * half + 2)),
            dma((NX,)), dma((NX,)), dma((2,)),
        ],
        compiler_params=pltpu.CompilerParams(
            collective_id=0, has_side_effects=True, vmem_limit_bytes=56 * 1024 * 1024
        ),
    )(
        line(owner_map), line(row_index), line(bag_index),
        line(prev_owner), line(prev_row), line(prev_bag),
        grad_pooled.reshape(bags, width), row_accum.reshape(rows_dev // nb, nb), item_table,
    )
    return (
        pooled.reshape(1, 1, bags, width),
        new_table,
        new_accum.reshape(rows_dev),
    )


def solution(mesh):
    ny, nz = mesh.shape["dp"] // 2, mesh.shape["rows"] // NX
    placed = (
        P("rows", None),
        P("rows"),
        P("dp", "rows", None, None),
        P("dp", "rows", None),
        P("dp", "rows", None),
        P("dp", "rows", None, None),
        P("dp", "rows", None),
        P("dp", "rows", None),
        P("dp", "rows", None, None),
    )
    return jax.shard_map(
        functools.partial(local, ny, nz),
        mesh=mesh,
        in_specs=placed,
        out_specs=(P("dp", "rows", None, None), P("rows", None), P("rows")),
        check_vma=False,
    )
```

```python
import functools

import jax
import jax.numpy as jnp
from jax import lax
from jax.experimental import pallas as pl
from jax.experimental.pallas import tpu as pltpu
from jax.sharding import PartitionSpec as P

learn_rate = 0.1
CAP = 24
NX = 4
MESH = pl.DeviceIdType.MESH
F32, BF16, I32 = jnp.float32, jnp.bfloat16, jnp.int32
NT = (((1,), (1,)), ((), ()))
NN = (((1,), (0,)), ((), ()))


def dot(a, b, dims=NN):
    return lax.dot_general(a, b, dims, preferred_element_type=F32)


def iota(shape, axis):
    return lax.broadcasted_iota(I32, shape, axis)


def split(v):
    high = v.astype(BF16)
    return high, (v - high.astype(F32)).astype(BF16)


def one_hot(mask):
    return jnp.where(mask, 1.0, 0.0).astype(BF16)


def by_owner(owner, row, bag, powner, prow, pbag, nz):
    n = owner.shape[1]

    def owners(o):
        return iota((nz * 8, n), 0) == (o // NX) * 8 + o % NX

    now, old = owners(owner), owners(powner)
    before = one_hot(iota((n, n), 0) < iota((n, n), 1))
    count = dot(jnp.concatenate([one_hot(now), one_hot(old)], axis=0), before)

    def places(mask, count, row, bag):
        rank = jnp.sum(jnp.where(mask, count, 0.0), axis=0, keepdims=True)
        hit = iota((32, n), 0).astype(F32) == rank
        row = row + 1
        low, high, bag = (v.astype(F32) for v in (row % 128, row // 128, bag))
        pick = lambda v: jnp.where(hit, v, 0.0)
        return [pick(low), pick(bag)], [pick(high), jnp.zeros((32, n), F32)]

    none = [jnp.zeros((64, n), F32)]
    left, lows, highs = [], [], []
    for o, first, (low, high) in (
        (powner, 0, places(old, count[nz * 8:], prow, pbag)),
        (owner, 2, places(now, count[: nz * 8], row, bag)),
    ):
        x = o % NX
        line = (o // NX) * 8 + first + x // 2
        for side in range(2):
            left.append(one_hot((iota((nz * 8, n), 0) == line) & (x % 2 == side)))
            fill = lambda v: jnp.concatenate(v + none if side == 0 else none + v, axis=0)
            lows.append(fill(low).astype(BF16))
            highs.append(fill(high).astype(BF16))
    left, lows, highs = (jnp.concatenate(v, axis=1) for v in (left, lows, highs))
    return dot(left, lows, NT) + 128.0 * dot(left, highs, NT)


def kernel(
    ny, nz,
    owner, row, bag, powner, prow, pbag, grad, accum, table,
    pooled, new_table, new_accum,
    idbuf, gradbuf, accbuf, in_sem, tab, tabs, zsend, zbuf, z2send, z2buf, xsend, xbuf, x2send, x2buf,
    expand, hits, look, part, psend, pbuf, qsend, qbuf, u, rbuf, gall,
    tab_sem, z_sem, z2_sem, x_send, x_recv, x2_send, x2_recv, c_send, c_recv,
    rs_send, rs_recv, ag_send, ag_recv, k_send, k_recv, px_send, px_recv, pz_sem,
):
    dp, rw = lax.axis_index("dp"), lax.axis_index("rows")
    y, c, z, x = dp // 2, dp % 2, rw // NX, rw % NX
    ns = NX * nz
    rows_dev = tab.shape[0]
    half_rows = rows_dev // 2
    nb = half_rows // ny
    nh = nb // 2
    gt = nz * 8

    def at(dp_, rw_):
        return {"dp": dp_, "rows": rw_}

    def far_first(i):
        return nz // 2 + (i % 2) * ((i + 1) // 2) - (1 - i % 2) * (i // 2)

    def z_peer(d):
        return at(dp, ((z + d) % nz) * NX + x)

    def x_peer(d):
        return at(dp, z * NX + (x + d) % NX)

    partner = at(y * 2 + 1 - c, rw)
    y_peer = [at(((y + 1) % ny) * 2 + c, rw), at(((y + ny - 1) % ny) * 2 + c, rw)]

    def remote(src, dst, s, r, dev):
        return pltpu.make_async_remote_copy(
            src_ref=src, dst_ref=dst, send_sem=s, recv_sem=r, device_id=dev, device_id_type=MESH
        )

    barrier = pltpu.get_barrier_semaphore()

    def greet(i, _):
        pl.semaphore_signal(barrier, inc=1, device_id=z_peer(far_first(i)), device_id_type=MESH)
        return 0

    lax.fori_loop(0, nz - 1, greet, 0)
    for d in range(1, NX):
        pl.semaphore_signal(barrier, inc=1, device_id=x_peer(d), device_id_type=MESH)
    for dev in [partner] + y_peer:
        pl.semaphore_signal(barrier, inc=1, device_id=dev, device_id_type=MESH)

    firsts = [
        pltpu.make_async_copy(src, idbuf.at[i], in_sem.at[i])
        for i, src in enumerate((powner, prow, pbag, owner, row, bag))
    ]
    firsts.append(pltpu.make_async_copy(grad, gradbuf, in_sem.at[6]))
    for copy in firsts:
        copy.start()
    loads = [
        pltpu.make_async_copy(accum, accbuf, in_sem.at[7]),
        pltpu.make_async_copy(table, tab, tab_sem),
    ]
    for copy in loads:
        copy.start()
    for copy in firsts:
        copy.wait()
    message = by_owner(
        idbuf[3], idbuf[4], idbuf[5], idbuf[0], idbuf[1], idbuf[2], nz
    )
    g4 = gradbuf[...]
    tile = jnp.concatenate([g4[:, :128], g4[:, 128:]], axis=0)
    for i in range(nz):
        zsend[i, 0:8, :] = tile
        zsend[i, 8:10, :] = message[i * 8:i * 8 + 2]
        z2send[i] = message[i * 8 + 2:i * 8 + 4]
    pl.semaphore_wait(barrier, nz - 1 + NX - 1 + 1 + 2)

    def send_z(i, _):
        d = far_first(i)
        to = (z + d) % nz
        remote(zsend.at[to], zbuf.at[z], z_sem.at[0], z_sem.at[1], z_peer(d)).start()
        return 0

    def send_z2(i, _):
        d = far_first(i)
        to = (z + d) % nz
        remote(z2send.at[to], z2buf.at[z], z2_sem.at[0], z2_sem.at[1], z_peer(d)).start()
        return 0

    def from_others(buf, sems):
        others = buf.at[pl.ds(0, nz - 1)]
        return remote(others, others, sems.at[0], sems.at[1], z_peer(1))

    lax.fori_loop(0, nz - 1, send_z, 0)
    lax.fori_loop(0, nz - 1, send_z2, 0)
    zbuf[z] = zsend[z]
    z2buf[z] = z2send[z]
    z_all, z2_all = from_others(zbuf, z_sem), from_others(z2buf, z2_sem)
    z_all.wait_recv()

    for i in range(NX):
        for j in range(nz):
            xsend[i, j * 8:(j + 1) * 8, :] = zbuf[j, 0:8, :]
        xsend[i, gt:gt + nz, :] = zbuf[:, 8 + i // 2, :]
    x_copies = []
    for d in range(1, NX):
        x_copies.append(
            remote(xsend.at[(x + d) % NX], xbuf.at[c, x], x_send.at[d], x_recv.at[d], x_peer(d))
        )
        x_copies[-1].start()
    xbuf[c, x] = xsend[x]
    own = xbuf.at[c, x]
    c_copies = [remote(own, own, c_send.at[0], c_recv.at[0], partner)]
    c_copies[0].start()
    z2_all.wait_recv()
    for i in range(NX):
        x2send[i] = z2buf[:, i // 2, :]
    x2_copies = []
    for d in range(1, NX):
        x2_copies.append(
            remote(x2send.at[(x + d) % NX], x2buf.at[x], x2_send.at[d], x2_recv.at[d], x_peer(d))
        )
        x2_copies[-1].start()
    x2buf[x] = x2send[x]
    for d in range(1, NX):
        x_copies[d - 1].wait_recv()
        piece = xbuf.at[c, (x + NX - d) % NX]
        c_copies.append(remote(piece, piece, c_send.at[d], c_recv.at[d], partner))
        c_copies[-1].start()

    for copy in loads:
        copy.wait()
    high, low = split(tab[...])
    tabs[:, 0:256] = high
    tabs[:, 256:512] = low
    for copy in c_copies:
        copy.wait_recv()

    def own_lanes(v):
        return jnp.where(x % 2 == 0, v, pltpu.roll(v, 64, 1))

    ids = own_lanes(
        jnp.concatenate([xbuf[i, j, gt:gt + nz, :] for i in range(2) for j in range(NX)], axis=0)
    )
    lines = 2 * ns
    grads = []
    for b in range(4):
        sides = [
            jnp.concatenate(
                [
                    xbuf[i, j, pl.ds(b + 4 * h, nz, stride=8), :]
                    for i in range(2)
                    for j in range(NX)
                ],
                axis=0,
            )
            for h in range(2)
        ]
        grads.append(jnp.concatenate(sides, axis=1))
    for k in range(CAP):
        of = ids[:, 32 + k:33 + k]
        each = jnp.where(of < 0.5, grads[0], jnp.where(of < 1.5, grads[1], jnp.where(of < 2.5, grads[2], grads[3])))
        high, low = split(each)
        expand[k * lines:(k + 1) * lines, 0:256] = high
        expand[k * lines:(k + 1) * lines, 256:512] = low
    keys = ids.T[0:CAP]

    def sums(offsets):
        for i, d in enumerate(offsets):
            base = c * half_rows + ((y + d + ny) % ny) * nb + 1
            number = (iota((nb, lines), 0) + base).astype(F32)
            for k in range(CAP):
                hits[i * nb:(i + 1) * nb, k * lines:(k + 1) * lines] = one_hot(number == keys[k:k + 1, :])
        both = dot(hits[...], expand[...])
        total = both[:, 0:256] + both[:, 256:512]
        for i, d in enumerate(offsets):
            u[(d + ny) % ny] = total[i * nb:(i + 1) * nb]

    slots = CAP // 3

    def look_up(first):
        if first == 0:
            for copy in x2_copies:
                copy.wait_recv()
        mine = own_lanes(jnp.concatenate([x2buf[j] for j in range(NX)], axis=0))
        for k in range(slots):
            col = mine[:, first + k:first + k + 1]
            number = (iota((ns, rows_dev), 1) + 1).astype(F32)
            look[k * ns:(k + 1) * ns, :] = one_hot(number == col)
        both = dot(look[...], tabs[...])
        found = both[:, 0:256] + both[:, 256:512]
        for b in range(4):
            total = jnp.zeros((ns, 256), F32) if first == 0 else part[b]
            for k in range(slots):
                of = mine[:, 32 + first + k:33 + first + k]
                total = total + jnp.where(of == b, found[k * ns:(k + 1) * ns], 0.0)
            part[b] = total

    def cut(ref, h):
        return ref.at[pl.ds(h * nh, nh)]

    half = ny // 2
    pieces = [(1, 0)] + [(t, h) for t in range(2, half + 1) for h in (1, 0)]
    number_of = {piece: i for i, piece in enumerate(pieces)}
    rs_copies = {}

    def rs_copy(way, t, h):
        i = number_of[(t, h)]
        d = half + 1 - t
        src = cut(u.at[d if way == 0 else (ny - d) % ny], h if way == 0 else 1 - h)
        copy = remote(src, rbuf.at[way, i], rs_send.at[way, i], rs_recv.at[way, i], y_peer[way])
        rs_copies[way, t, h] = copy
        copy.start()

    def rs_take(way, t, h):
        rs_copies[way, t, h].wait_recv()
        i = number_of[(t, h)]
        d = half - t
        hh = h if way == 0 else 1 - h
        slot = d if way == 0 else (ny - d) % ny
        rows = pl.ds(hh * nh, nh)
        u[slot, rows, :] = u[slot, rows, :] + rbuf[way, i]

    px_copies = []

    def pool_x():
        for b in range(4):
            total = part[b]
            for h in range(2):
                psend[pl.ds(b + 4 * h, ns, stride=8), :] = total[:, h * 128:(h + 1) * 128]
        for d in range(1, NX):
            src = psend.at[pl.ds(((x + d) % NX) * gt, gt)]
            px_copies.append(remote(src, pbuf.at[d], px_send.at[d], px_recv.at[d], x_peer(d)))
            px_copies[-1].start()

    rest = [functools.partial(sums, (half + 1 - t, t - half - 1)) for t in range(2, half + 1)]
    rest += [functools.partial(look_up, i * slots) for i in range(3)] + [pool_x]

    def between():
        if rest:
            rest.pop(0)()

    sums((half, 0))
    for way in range(2):
        rs_copy(way, 1, 0)
    between()
    for way in range(2):
        rs_copy(way, 2, 1)
    between()
    for t, h in pieces[:-2]:
        for way in range(2):
            rs_take(way, t, h)
            rs_copy(way, t + 1, h)
        between()
    while rest:
        between()
    for t, h in pieces[-2:]:
        for way in range(2):
            rs_take(way, t, h)

    def block(line, core, h):
        first = core * half_rows + line * nb
        return pl.ds(first, nb) if h is None else pl.ds(first + h * nh, nh)

    def from_line(way, t):
        return (y + ny - t) % ny if way == 0 else (y + t) % ny

    ag_copies, k_copies = {}, {}

    def ag_copy(way, t, h):
        rows = gall.at[block(from_line(way, t - 1), c, h)]
        i = (t - 1) * 2 + h
        ag_copies[way, t, h] = remote(rows, rows, ag_send.at[way, i], ag_recv.at[way, i], y_peer[way])
        ag_copies[way, t, h].start()

    def core_copy(way, t, h):
        rows = gall.at[block(from_line(way, t), c, h)]
        k_copies[way, t] = remote(rows, rows, k_send.at[way, t], k_recv.at[way, t], partner)
        k_copies[way, t].start()

    def update(way, t, h, core):
        line = from_line(way, t)
        rows = block(line, core, h)
        g = gall[rows, :]
        n = g.shape[0]
        at_row = core * ny + line
        eye = iota((n, nb), 0) + (h or 0) * nh == iota((n, nb), 1)
        before = jnp.sum(jnp.where(eye, accbuf[pl.ds(at_row, 1), :], 0.0), axis=1, keepdims=True)
        after = before + jnp.sum(g * g, axis=1, keepdims=True) * (1.0 / g.shape[1])
        new_table[rows, :] = tab[rows, :] - learn_rate * g / jnp.sqrt(after)
        line_after = jnp.sum(jnp.where(eye, after, 0.0), axis=0, keepdims=True)
        if h == 1:
            line_after = line_after + new_accum[pl.ds(at_row, 1), :]
        new_accum[pl.ds(at_row, 1), :] = line_after

    gall[block(y, c, None), :] = u[0]
    for h in range(2):
        for way in range(2):
            ag_copy(way, 1, h if way == 0 else 1 - h)
    core_copy(0, 0, None)

    def pool_z():
        for copy in px_copies:
            copy.wait_recv()
        total = psend[pl.ds(x * gt, gt), :]
        for d in range(1, NX):
            total = total + pbuf[d]
        for i in range(nz):
            qsend[i] = total[i * 8:(i + 1) * 8]
        qbuf[z] = qsend[z]
        lax.fori_loop(0, nz // 2, send_q, 0)

    def pool_z_rest():
        lax.fori_loop(nz // 2, nz - 1, send_q, 0)

    def send_q(i, _):
        d = far_first(i)
        to = (z + d) % nz
        remote(qsend.at[to], qbuf.at[z], pz_sem.at[0], pz_sem.at[1], z_peer(d)).start()
        return 0

    q_all = from_others(qbuf, pz_sem)

    def sent(copies):
        for copy in copies:
            copy.wait_send()

    def update_all(jobs):
        for job in jobs:
            update(*job)

    def update_other(jobs):
        for way, t, h in jobs:
            k_copies[way, t].wait_recv()
            update(way, t, h, 1 - c)

    meanwhile = {
        (1, 0): [lambda: update(0, 0, None, c)],
        (1, 1): [pool_z],
        (2, 0): [pool_z_rest, lambda: sent((z_all, z2_all, *x_copies, *x2_copies, *c_copies))],
    }
    own = lambda t: [(way, t, None, c) for way in range(2)]
    other = lambda t: [(way, t, None) for way in range(2)]
    for t in range(1, half):
        for h in range(2):
            for way in range(2):
                hh = h if way == 0 else 1 - h
                ag_copies[way, t, hh].wait_recv()
                if t + 1 < half or hh == way:
                    ag_copy(way, t + 1, hh)
                if h == 1:
                    core_copy(way, t, None)
            for job in meanwhile.pop((t, h), []):
                job()
            if h == 0 and t > 1:
                update_all(own(t - 1))
            if h == 1:
                update_other(other(t - 1) if t > 1 else [(0, 0, None)])
    for jobs in meanwhile.values():
        for job in jobs:
            job()
    update_all(own(half - 1))
    sent((*px_copies, *rs_copies.values()))
    for way in range(2):
        ag_copies[way, half, way].wait_recv()
        core_copy(way, half, way)
    update_other(other(half - 1))
    for way in range(2):
        update(way, half, way, c)
    q_all.wait_recv()
    total = qbuf[0]
    for i in range(1, nz):
        total = total + qbuf[i]
    pooled[:, 0:128] = total[0:4]
    pooled[:, 128:256] = total[4:8]
    sent((q_all, *ag_copies.values()))
    for way in range(2):
        k_copies[way, half].wait_recv()
        update(way, half, way, 1 - c)
    sent(k_copies.values())


def hand_on(pooled, new_table, new_accum, pooled_out, table_out, accum_out, sems):
    copies = [
        pltpu.make_async_copy(src, dst, sems.at[i])
        for i, (src, dst) in enumerate(
            ((new_table, table_out), (pooled, pooled_out), (new_accum, accum_out))
        )
    ]
    for copy in copies:
        copy.start()
    for copy in copies:
        copy.wait()


def local(
    ny, nz,
    item_table, row_accum, owner_map, row_index, bag_index, prev_owner, prev_row, prev_bag, grad_pooled,
):
    rows_dev, width = item_table.shape
    bags = grad_pooled.shape[2]
    n = row_index.shape[2]
    half_rows = rows_dev // 2
    nb = half_rows // ny
    nh = nb // 2
    ns, gt, half = NX * nz, nz * 8, ny // 2
    lines = 2 * ns
    line = lambda a: a.reshape(1, n)
    vmem = pl.BlockSpec(memory_space=pltpu.VMEM)
    hbm = pl.BlockSpec(memory_space=pl.ANY)
    dma = pltpu.SemaphoreType.DMA
    sums = [
        ((bags, width), F32),
        ((rows_dev, width), F32),
        ((rows_dev // nb, nb), F32),
    ]
    inputs = (
        *(line(v) for v in (owner_map, row_index, bag_index, prev_owner, prev_row, prev_bag)),
        grad_pooled.reshape(bags, width), row_accum.reshape(rows_dev // nb, nb), item_table,
    )
    results = pl.pallas_call(
        functools.partial(kernel, ny, nz),
        out_shape=[jax.ShapeDtypeStruct(*s) for s in sums],
        in_specs=[pl.BlockSpec(memory_space=pltpu.HBM)] * 9,
        out_specs=[vmem] * 3,
        scratch_shapes=[
            pltpu.VMEM((6, 1, n), I32),
            pltpu.VMEM((bags, width), F32),
            pltpu.VMEM((rows_dev // nb, nb), F32),
            dma((8,)),
            pltpu.VMEM((rows_dev, width), F32),
            pltpu.VMEM((rows_dev, 2 * width), BF16),
            pltpu.VMEM((nz, 10, 128), F32),
            pltpu.VMEM((nz, 10, 128), F32),
            pltpu.VMEM((nz, 2, 128), F32),
            pltpu.VMEM((nz, 2, 128), F32),
            pltpu.VMEM((NX, gt + nz, 128), F32),
            pltpu.VMEM((2, NX, gt + nz, 128), F32),
            pltpu.VMEM((NX, nz, 128), F32),
            pltpu.VMEM((NX, nz, 128), F32),
            pltpu.VMEM((CAP * lines, 2 * width), BF16),
            pltpu.VMEM((2 * nb, CAP * lines), BF16),
            pltpu.VMEM((CAP // 3 * ns, rows_dev), BF16),
            pltpu.VMEM((4, ns, width), F32),
            pltpu.VMEM((ns * 8, 128), F32),
            pltpu.VMEM((NX, gt, 128), F32),
            pltpu.VMEM((nz, 8, 128), F32),
            pltpu.VMEM((nz, 8, 128), F32),
            pltpu.VMEM((ny, nb, width), F32),
            pltpu.VMEM((2, 2 * half - 1, nh, width), F32),
            pltpu.VMEM((rows_dev, width), F32),
            dma(()), dma((2,)), dma((2,)),
            dma((NX,)), dma((NX,)), dma((NX,)), dma((NX,)), dma((NX,)), dma((NX,)),
            dma((2, 2 * half)), dma((2, 2 * half)),
            dma((2, 2 * half)), dma((2, 2 * half)),
            dma((2, half + 1)), dma((2, half + 1)),
            dma((NX,)), dma((NX,)), dma((2,)),
        ],
        compiler_params=pltpu.CompilerParams(
            collective_id=0, has_side_effects=True, vmem_limit_bytes=40 * 1024 * 1024
        ),
    )(
        *(pltpu.with_memory_space_constraint(v, pltpu.HBM) for v in inputs)
    )
    pooled, new_table, new_accum = pl.pallas_call(
        hand_on,
        out_shape=[jax.ShapeDtypeStruct(*s) for s in sums],
        in_specs=[vmem] * 3,
        out_specs=[hbm] * 3,
        scratch_shapes=[dma((3,))],
        compiler_params=pltpu.CompilerParams(vmem_limit_bytes=4 * 1024 * 1024),
    )(*results)
    return (
        pooled.reshape(1, 1, bags, width),
        new_table,
        new_accum.reshape(rows_dev),
    )


def solution(mesh):
    ny, nz = mesh.shape["dp"] // 2, mesh.shape["rows"] // NX
    placed = (
        P("rows", None),
        P("rows"),
        P("dp", "rows", None, None),
        P("dp", "rows", None),
        P("dp", "rows", None),
        P("dp", "rows", None, None),
        P("dp", "rows", None),
        P("dp", "rows", None),
        P("dp", "rows", None, None),
    )
    return jax.shard_map(
        functools.partial(local, ny, nz),
        mesh=mesh,
        in_specs=placed,
        out_specs=(P("dp", "rows", None, None), P("rows", None), P("rows")),
        check_vma=False,
    )
```

```python
import functools

import jax
import jax.numpy as jnp
from jax import lax
from jax.experimental import pallas as pl
from jax.experimental.pallas import tpu as pltpu
from jax.sharding import PartitionSpec as P

learn_rate = 0.1
CAP = 24
NX = 4
MESH = pl.DeviceIdType.MESH
F32, BF16, I32 = jnp.float32, jnp.bfloat16, jnp.int32
NT = (((1,), (1,)), ((), ()))
NN = (((1,), (0,)), ((), ()))


def dot(a, b, dims=NN):
    return lax.dot_general(a, b, dims, preferred_element_type=F32)


def iota(shape, axis):
    return lax.broadcasted_iota(I32, shape, axis)


def split(v):
    high = v.astype(BF16)
    return high, (v - high.astype(F32)).astype(BF16)


def one_hot(mask):
    return jnp.where(mask, 1.0, 0.0).astype(BF16)


def by_owner(owner, row, bag, powner, prow, pbag, nz):
    n = owner.shape[1]

    def owners(o):
        return iota((nz * 8, n), 0) == (o // NX) * 8 + o % NX

    now, old = owners(owner), owners(powner)
    before = one_hot(iota((n, n), 0) < iota((n, n), 1))
    count = dot(jnp.concatenate([one_hot(now), one_hot(old)], axis=0), before)

    def places(mask, count, row, bag):
        rank = jnp.sum(jnp.where(mask, count, 0.0), axis=0, keepdims=True)
        hit = iota((32, n), 0).astype(F32) == rank
        row = row + 1
        low, high, bag = (v.astype(F32) for v in (row % 128, row // 128, bag))
        pick = lambda v: jnp.where(hit, v, 0.0)
        return [pick(low), pick(bag)], [pick(high), jnp.zeros((32, n), F32)]

    none = [jnp.zeros((64, n), F32)]
    left, lows, highs = [], [], []
    for o, first, (low, high) in (
        (powner, 0, places(old, count[nz * 8:], prow, pbag)),
        (owner, 2, places(now, count[: nz * 8], row, bag)),
    ):
        x = o % NX
        line = (o // NX) * 8 + first + x // 2
        for side in range(2):
            left.append(one_hot((iota((nz * 8, n), 0) == line) & (x % 2 == side)))
            fill = lambda v: jnp.concatenate(v + none if side == 0 else none + v, axis=0)
            lows.append(fill(low).astype(BF16))
            highs.append(fill(high).astype(BF16))
    left, lows, highs = (jnp.concatenate(v, axis=1) for v in (left, lows, highs))
    return dot(left, lows, NT) + 128.0 * dot(left, highs, NT)


def kernel(
    ny, nz,
    owner, row, bag, powner, prow, pbag, grad, accum, table,
    pooled, new_table, new_accum,
    idbuf, gradbuf, accbuf, in_sem, tab, tabs, zsend, zbuf, xsend, xbuf, x2send, x2buf,
    expand, hits, look, part, psend, pbuf, qsend, qbuf, u, rbuf, gall,
    tab_sem, z_sem, x_send, x_recv, x2_send, x2_recv, c_send, c_recv,
    rs_send, rs_recv, ag_send, ag_recv, k_send, k_recv, px_send, px_recv, pz_sem,
):
    dp, rw = lax.axis_index("dp"), lax.axis_index("rows")
    y, c, z, x = dp // 2, dp % 2, rw // NX, rw % NX
    ns = NX * nz
    rows_dev = tab.shape[0]
    half_rows = rows_dev // 2
    nb = half_rows // ny
    nh = nb // 2
    gt = nz * 8

    def at(dp_, rw_):
        return {"dp": dp_, "rows": rw_}

    def far_first(i):
        return nz // 2 + (i % 2) * ((i + 1) // 2) - (1 - i % 2) * (i // 2)

    def z_peer(d):
        return at(dp, ((z + d) % nz) * NX + x)

    def x_peer(d):
        return at(dp, z * NX + (x + d) % NX)

    partner = at(y * 2 + 1 - c, rw)
    y_peer = [at(((y + 1) % ny) * 2 + c, rw), at(((y + ny - 1) % ny) * 2 + c, rw)]

    def remote(src, dst, s, r, dev):
        return pltpu.make_async_remote_copy(
            src_ref=src, dst_ref=dst, send_sem=s, recv_sem=r, device_id=dev, device_id_type=MESH
        )

    barrier = pltpu.get_barrier_semaphore()

    def greet(i, _):
        pl.semaphore_signal(barrier, inc=1, device_id=z_peer(far_first(i)), device_id_type=MESH)
        return 0

    lax.fori_loop(0, nz - 1, greet, 0)
    for d in range(1, NX):
        pl.semaphore_signal(barrier, inc=1, device_id=x_peer(d), device_id_type=MESH)
    for dev in [partner] + y_peer:
        pl.semaphore_signal(barrier, inc=1, device_id=dev, device_id_type=MESH)

    firsts = [
        pltpu.make_async_copy(src, idbuf.at[i], in_sem.at[i])
        for i, src in enumerate((powner, prow, pbag, owner, row, bag))
    ]
    firsts.append(pltpu.make_async_copy(grad, gradbuf, in_sem.at[6]))
    for copy in firsts:
        copy.start()
    loads = [
        pltpu.make_async_copy(accum, accbuf, in_sem.at[7]),
        pltpu.make_async_copy(table, tab, tab_sem),
    ]
    for copy in loads:
        copy.start()
    for copy in firsts:
        copy.wait()
    message = by_owner(
        idbuf[3], idbuf[4], idbuf[5], idbuf[0], idbuf[1], idbuf[2], nz
    )
    g4 = gradbuf[...]
    tile = jnp.concatenate([g4[:, :128], g4[:, 128:]], axis=0)
    for i in range(nz):
        zsend[i, 0:8, :] = tile
        zsend[i, 8:12, :] = message[i * 8:i * 8 + 4]
    pl.semaphore_wait(barrier, nz - 1 + NX - 1 + 1 + 2)

    def send_z(i, _):
        d = far_first(i)
        to = (z + d) % nz
        remote(zsend.at[to], zbuf.at[z], z_sem.at[0], z_sem.at[1], z_peer(d)).start()
        return 0

    def from_others(buf, sems):
        others = buf.at[pl.ds(0, nz - 1)]
        return remote(others, others, sems.at[0], sems.at[1], z_peer(1))

    lax.fori_loop(0, nz - 1, send_z, 0)
    zbuf[z] = zsend[z]
    z_all = from_others(zbuf, z_sem)

    for copy in loads:
        copy.wait()
    high, low = split(tab[...])
    tabs[:, 0:256] = high
    tabs[:, 256:512] = low
    z_all.wait_recv()

    for i in range(NX):
        x2send[i] = zbuf[:, 10 + i // 2, :]
    x2_copies = []
    for d in range(1, NX):
        x2_copies.append(
            remote(x2send.at[(x + d) % NX], x2buf.at[x], x2_send.at[d], x2_recv.at[d], x_peer(d))
        )
        x2_copies[-1].start()
    for i in range(NX):
        for j in range(nz):
            xsend[i, j * 8:(j + 1) * 8, :] = zbuf[j, 0:8, :]
        xsend[i, gt:gt + nz, :] = zbuf[:, 8 + i // 2, :]
    x_copies = []
    for d in (2, 1, 3):
        x_copies.append(
            remote(xsend.at[(x + d) % NX], xbuf.at[c, x], x_send.at[d], x_recv.at[d], x_peer(d))
        )
        x_copies[-1].start()
    xbuf[c, x] = xsend[x]
    own = xbuf.at[c, x]
    c_copies = [remote(own, own, c_send.at[0], c_recv.at[0], partner)]
    c_copies[0].start()
    x2buf[x] = x2send[x]

    def own_lanes(v):
        return jnp.where(x % 2 == 0, v, pltpu.roll(v, 64, 1))

    slots = CAP // 3

    def look_up(first):
        if first == 0:
            for copy in x2_copies:
                copy.wait_recv()
        mine = own_lanes(jnp.concatenate([x2buf[j] for j in range(NX)], axis=0))
        for k in range(slots):
            col = mine[:, first + k:first + k + 1]
            number = (iota((ns, rows_dev), 1) + 1).astype(F32)
            look[k * ns:(k + 1) * ns, :] = one_hot(number == col)
        both = dot(look[...], tabs[...])
        found = both[:, 0:256] + both[:, 256:512]
        for b in range(4):
            total = jnp.zeros((ns, 256), F32) if first == 0 else part[b]
            for k in range(slots):
                of = mine[:, 32 + first + k:33 + first + k]
                total = total + jnp.where(of == b, found[k * ns:(k + 1) * ns], 0.0)
            part[b] = total

    look_up(0)

    lines = 2 * ns

    def expand_piece(i, j):
        ids = own_lanes(xbuf[i, j, gt:gt + nz, :])
        grads = [
            jnp.concatenate(
                [xbuf[i, j, pl.ds(b + 4 * h, nz, stride=8), :] for h in range(2)], axis=1
            )
            for b in range(4)
        ]
        for k in range(CAP):
            of = ids[:, 32 + k:33 + k]
            low_half = jnp.where(of < 0.5, grads[0], grads[1])
            high, low = split(jnp.where(of < 1.5, low_half, jnp.where(of < 2.5, grads[2], grads[3])))
            expand[k, i * NX + j, :, 0:256] = high
            expand[k, i * NX + j, :, 256:512] = low

    expand_piece(c, x)
    for n, d in enumerate((1, 3, 2)):
        x_copies[(2, 1, 3).index(d)].wait_recv()
        piece = xbuf.at[c, (x + NX - d) % NX]
        c_copies.append(remote(piece, piece, c_send.at[d], c_recv.at[d], partner))
        c_copies[-1].start()
        if n > 0:
            expand_piece(c, (x + NX - (1, 3, 2)[n - 1]) % NX)
    expand_piece(c, (x + NX - 2) % NX)
    for copy, d in zip(c_copies, (0, 1, 3, 2)):
        copy.wait_recv()
        expand_piece(1 - c, (x + NX - d) % NX)
    ids = own_lanes(
        jnp.concatenate([xbuf[i, j, gt:gt + nz, :] for i in range(2) for j in range(NX)], axis=0)
    )
    keys = ids.T[0:CAP]

    def sums(offsets):
        for i, d in enumerate(offsets):
            base = c * half_rows + ((y + d + ny) % ny) * nb + 1
            number = (iota((nb, lines), 0) + base).astype(F32)
            for k in range(CAP):
                hits[i * nb:(i + 1) * nb, k * lines:(k + 1) * lines] = one_hot(number == keys[k:k + 1, :])
        many = len(offsets) * nb
        both = dot(hits[0:many], expand[...].reshape(CAP * lines, expand.shape[-1]))
        total = both[:, 0:256] + both[:, 256:512]
        for i, d in enumerate(offsets):
            u[(d + ny) % ny] = total[i * nb:(i + 1) * nb]

    def cut(ref, h):
        return ref.at[pl.ds(h * nh, nh)]

    half = ny // 2
    pieces = [(1, 0)] + [(t, h) for t in range(2, half + 1) for h in (1, 0)]
    number_of = {piece: i for i, piece in enumerate(pieces)}
    rs_copies = {}

    def rs_copy(way, t, h):
        i = number_of[(t, h)]
        d = half + 1 - t
        src = cut(u.at[d if way == 0 else (ny - d) % ny], h if way == 0 else 1 - h)
        copy = remote(src, rbuf.at[way, i], rs_send.at[way, i], rs_recv.at[way, i], y_peer[way])
        rs_copies[way, t, h] = copy
        copy.start()

    def rs_take(way, t, h):
        rs_copies[way, t, h].wait_recv()
        i = number_of[(t, h)]
        d = half - t
        hh = h if way == 0 else 1 - h
        slot = d if way == 0 else (ny - d) % ny
        rows = pl.ds(hh * nh, nh)
        u[slot, rows, :] = u[slot, rows, :] + rbuf[way, i]

    px_copies = []

    def pool_x():
        for b in range(4):
            total = part[b]
            for h in range(2):
                psend[pl.ds(b + 4 * h, ns, stride=8), :] = total[:, h * 128:(h + 1) * 128]
        for d in range(1, NX):
            src = psend.at[pl.ds(((x + d) % NX) * gt, gt)]
            px_copies.append(remote(src, pbuf.at[d], px_send.at[d], px_recv.at[d], x_peer(d)))
            px_copies[-1].start()

    rest = [functools.partial(sums, (half + 1 - t, t - half - 1)) for t in range(2, half + 1)]
    rest += [functools.partial(look_up, i * slots) for i in (1, 2)] + [lambda: (pool_x(), sums((0,)))]

    def between():
        if rest:
            rest.pop(0)()

    sums((half,))
    for way in range(2):
        rs_copy(way, 1, 0)
    between()
    for way in range(2):
        rs_copy(way, 2, 1)
    between()
    for t, h in pieces[:-2]:
        for way in range(2):
            rs_take(way, t, h)
            rs_copy(way, t + 1, h)
        between()
    while rest:
        between()
    for t, h in pieces[-2:]:
        for way in range(2):
            rs_take(way, t, h)

    def block(line, core, h):
        first = core * half_rows + line * nb
        return pl.ds(first, nb) if h is None else pl.ds(first + h * nh, nh)

    def from_line(way, t):
        return (y + ny - t) % ny if way == 0 else (y + t) % ny

    ag_copies, k_copies = {}, {}

    def ag_copy(way, t, h):
        rows = gall.at[block(from_line(way, t - 1), c, h)]
        i = (t - 1) * 2 + h
        ag_copies[way, t, h] = remote(rows, rows, ag_send.at[way, i], ag_recv.at[way, i], y_peer[way])
        ag_copies[way, t, h].start()

    def core_copy(way, t, h):
        rows = gall.at[block(from_line(way, t), c, h)]
        k_copies[way, t] = remote(rows, rows, k_send.at[way, t], k_recv.at[way, t], partner)
        k_copies[way, t].start()

    def update(way, t, h, core):
        line = from_line(way, t)
        rows = block(line, core, h)
        g = gall[rows, :]
        n = g.shape[0]
        at_row = core * ny + line
        eye = iota((n, nb), 0) + (h or 0) * nh == iota((n, nb), 1)
        before = jnp.sum(jnp.where(eye, accbuf[pl.ds(at_row, 1), :], 0.0), axis=1, keepdims=True)
        after = before + jnp.sum(g * g, axis=1, keepdims=True) * (1.0 / g.shape[1])
        new_table[rows, :] = tab[rows, :] - learn_rate * g / jnp.sqrt(after)
        line_after = jnp.sum(jnp.where(eye, after, 0.0), axis=0, keepdims=True)
        if h == 1:
            line_after = line_after + new_accum[pl.ds(at_row, 1), :]
        new_accum[pl.ds(at_row, 1), :] = line_after

    gall[block(y, c, None), :] = u[0]
    for h in range(2):
        for way in range(2):
            ag_copy(way, 1, h if way == 0 else 1 - h)
    core_copy(0, 0, None)

    def pool_z():
        for copy in px_copies:
            copy.wait_recv()
        total = psend[pl.ds(x * gt, gt), :]
        for d in range(1, NX):
            total = total + pbuf[d]
        for i in range(nz):
            qsend[i] = total[i * 8:(i + 1) * 8]
        qbuf[z] = qsend[z]
        lax.fori_loop(0, nz // 2, send_q, 0)

    def pool_z_rest():
        lax.fori_loop(nz // 2, nz - 1, send_q, 0)

    def send_q(i, _):
        d = far_first(i)
        to = (z + d) % nz
        remote(qsend.at[to], qbuf.at[z], pz_sem.at[0], pz_sem.at[1], z_peer(d)).start()
        return 0

    q_all = from_others(qbuf, pz_sem)

    def sent(copies):
        for copy in copies:
            copy.wait_send()

    def update_all(jobs):
        for job in jobs:
            update(*job)

    def update_other(jobs):
        for way, t, h in jobs:
            k_copies[way, t].wait_recv()
            update(way, t, h, 1 - c)

    meanwhile = {
        (1, 0): [lambda: update(0, 0, None, c)],
        (1, 1): [pool_z],
        (2, 0): [pool_z_rest, lambda: sent((z_all, *x_copies, *x2_copies, *c_copies))],
    }
    own = lambda t: [(way, t, None, c) for way in range(2)]
    other = lambda t: [(way, t, None) for way in range(2)]
    for t in range(1, half):
        for h in range(2):
            for way in range(2):
                hh = h if way == 0 else 1 - h
                ag_copies[way, t, hh].wait_recv()
                if t + 1 < half or hh == way:
                    ag_copy(way, t + 1, hh)
                if h == 1:
                    core_copy(way, t, None)
            for job in meanwhile.pop((t, h), []):
                job()
            if h == 0 and t > 1:
                update_all(own(t - 1))
            if h == 1:
                update_other(other(t - 1) if t > 1 else [(0, 0, None)])
    for jobs in meanwhile.values():
        for job in jobs:
            job()
    update_all(own(half - 1))
    sent((*px_copies, *rs_copies.values()))
    for way in range(2):
        ag_copies[way, half, way].wait_recv()
        core_copy(way, half, way)
    update_other(other(half - 1))
    for way in range(2):
        update(way, half, way, c)
    q_all.wait_recv()
    total = qbuf[0]
    for i in range(1, nz):
        total = total + qbuf[i]
    pooled[:, 0:128] = total[0:4]
    pooled[:, 128:256] = total[4:8]
    sent((q_all, *ag_copies.values()))
    for way in range(2):
        k_copies[way, half].wait_recv()
        update(way, half, way, 1 - c)
    sent(k_copies.values())


def hand_on(pooled, new_table, new_accum, pooled_out, table_out, accum_out, sems):
    copies = [
        pltpu.make_async_copy(src, dst, sems.at[i])
        for i, (src, dst) in enumerate(
            ((new_table, table_out), (pooled, pooled_out), (new_accum, accum_out))
        )
    ]
    for copy in copies:
        copy.start()
    for copy in copies:
        copy.wait()


def local(
    ny, nz,
    item_table, row_accum, owner_map, row_index, bag_index, prev_owner, prev_row, prev_bag, grad_pooled,
):
    rows_dev, width = item_table.shape
    bags = grad_pooled.shape[2]
    n = row_index.shape[2]
    half_rows = rows_dev // 2
    nb = half_rows // ny
    nh = nb // 2
    ns, gt, half = NX * nz, nz * 8, ny // 2
    lines = 2 * ns
    line = lambda a: a.reshape(1, n)
    vmem = pl.BlockSpec(memory_space=pltpu.VMEM)
    hbm = pl.BlockSpec(memory_space=pl.ANY)
    dma = pltpu.SemaphoreType.DMA
    sums = [
        ((bags, width), F32),
        ((rows_dev, width), F32),
        ((rows_dev // nb, nb), F32),
    ]
    inputs = (
        *(line(v) for v in (owner_map, row_index, bag_index, prev_owner, prev_row, prev_bag)),
        grad_pooled.reshape(bags, width), row_accum.reshape(rows_dev // nb, nb), item_table,
    )
    results = pl.pallas_call(
        functools.partial(kernel, ny, nz),
        out_shape=[jax.ShapeDtypeStruct(*s) for s in sums],
        in_specs=[pl.BlockSpec(memory_space=pltpu.HBM)] * 9,
        out_specs=[vmem] * 3,
        scratch_shapes=[
            pltpu.VMEM((6, 1, n), I32),
            pltpu.VMEM((bags, width), F32),
            pltpu.VMEM((rows_dev // nb, nb), F32),
            dma((8,)),
            pltpu.VMEM((rows_dev, width), F32),
            pltpu.VMEM((rows_dev, 2 * width), BF16),
            pltpu.VMEM((nz, 12, 128), F32),
            pltpu.VMEM((nz, 12, 128), F32),
            pltpu.VMEM((NX, gt + nz, 128), F32),
            pltpu.VMEM((2, NX, gt + nz, 128), F32),
            pltpu.VMEM((NX, nz, 128), F32),
            pltpu.VMEM((NX, nz, 128), F32),
            pltpu.VMEM((CAP, 2 * NX, nz, 2 * width), BF16),
            pltpu.VMEM((2 * nb, CAP * lines), BF16),
            pltpu.VMEM((CAP // 3 * ns, rows_dev), BF16),
            pltpu.VMEM((4, ns, width), F32),
            pltpu.VMEM((ns * 8, 128), F32),
            pltpu.VMEM((NX, gt, 128), F32),
            pltpu.VMEM((nz, 8, 128), F32),
            pltpu.VMEM((nz, 8, 128), F32),
            pltpu.VMEM((ny, nb, width), F32),
            pltpu.VMEM((2, 2 * half - 1, nh, width), F32),
            pltpu.VMEM((rows_dev, width), F32),
            dma(()), dma((2,)),
            dma((NX,)), dma((NX,)), dma((NX,)), dma((NX,)), dma((NX,)), dma((NX,)),
            dma((2, 2 * half)), dma((2, 2 * half)),
            dma((2, 2 * half)), dma((2, 2 * half)),
            dma((2, half + 1)), dma((2, half + 1)),
            dma((NX,)), dma((NX,)), dma((2,)),
        ],
        compiler_params=pltpu.CompilerParams(
            collective_id=0, has_side_effects=True, vmem_limit_bytes=40 * 1024 * 1024
        ),
    )(
        *(pltpu.with_memory_space_constraint(v, pltpu.HBM) for v in inputs)
    )
    pooled, new_table, new_accum = pl.pallas_call(
        hand_on,
        out_shape=[jax.ShapeDtypeStruct(*s) for s in sums],
        in_specs=[vmem] * 3,
        out_specs=[hbm] * 3,
        scratch_shapes=[dma((3,))],
        compiler_params=pltpu.CompilerParams(vmem_limit_bytes=4 * 1024 * 1024),
    )(*results)
    return (
        pooled.reshape(1, 1, bags, width),
        new_table,
        new_accum.reshape(rows_dev),
    )


def solution(mesh):
    ny, nz = mesh.shape["dp"] // 2, mesh.shape["rows"] // NX
    placed = (
        P("rows", None),
        P("rows"),
        P("dp", "rows", None, None),
        P("dp", "rows", None),
        P("dp", "rows", None),
        P("dp", "rows", None, None),
        P("dp", "rows", None),
        P("dp", "rows", None),
        P("dp", "rows", None, None),
    )
    return jax.shard_map(
        functools.partial(local, ny, nz),
        mesh=mesh,
        in_specs=placed,
        out_specs=(P("dp", "rows", None, None), P("rows", None), P("rows")),
        check_vma=False,
    )
```
